32 devices in a mesh: group: 4 (over x, core), blk: 8 (over z, y).
Axes of the slice: x: 2, y: 2, z: 4, core: 2. Of those that a mesh axis runs over, the one named last changes fastest.
Arguments:
- orbitals: float32 [32, 64, 4096], P(('group', 'blk')), may hold values from -6 to 6
- occupation: float32 [32], P(('group', 'blk')), may hold values from 0.3 to 1
Outputs:
- exchange: float32 [32, 64, 4096], P(('group', 'blk'))
The draws below stay inside these ranges and needn't reach their ends.
All inputs are finite; a program needn't handle non-finite values.
Results may differ from the reference program's by a relative error of at most 0.0003.
Values sent between devices are 32-bit elements; how exact they have to be, the bound alone decides.
A program may use at most 128 MiB of HBM per device.

```python
import jax
import jax.numpy as jnp
from jax import lax

GRID = 64
ORB_DEV = 1
STEPS = 3
ORBITALS = 32
N_GROUP = 4
N_BLK = 8


def block_scale(key, dims, shards, smallest, largest):
    def one(dim, parts):
        draws = jax.random.uniform(jax.random.fold_in(jax.random.fold_in(key, 6), dim), (parts,), jnp.float32, smallest / len(shards), largest / len(shards))
        return jnp.repeat(jnp.exp(draws), dims[dim] // parts).reshape((-1,) + (1,) * (len(dims) - dim - 1))

    gain = one(*shards[0])
    for cut in shards[1:]:
        gain = gain * one(*cut)
    return gain


def normal_values(stream_key, extent, width, reach, shards=(), kind=jnp.bfloat16):
    factor_of = block_scale(stream_key, extent, shards, -0.22, 0.18) if shards else 1.0
    values = jax.random.normal(stream_key, extent, jnp.float32) * width * factor_of
    return jnp.minimum(jnp.maximum(values, -reach), reach).astype(kind)


def setup_inputs(seed: int = 0) -> dict:
    keys = jax.random.split(jax.random.key(seed), 3)
    return {
        "orbitals": normal_values(keys[0], (ORBITALS, GRID, GRID * GRID), 1.0, 6.0, ((0, 32),), jnp.float32),
        "occupation": jnp.clip(0.3 + 0.7 * jax.random.uniform(keys[1], (ORBITALS,), jnp.float32) ** block_scale(keys[1], (ORBITALS,), ((0, 32),), -0.2, 0.2), 0.3, 1.0),
    }


def make_kernel(size):
    index = jnp.arange(size)
    signed = jnp.where(index < size // 2, index, index - size).astype(jnp.float32)
    square = signed * signed
    total = square[:, None, None] + square[None, :, None] + square[None, None, :]
    step = 2.0 * jnp.pi / size
    return jnp.pi / (step * step * total + 0.25)


def pair_terms(home, home_occ, visit, visit_occ, kernel):
    size = home.shape[1]
    count = home.shape[0]
    density = home[:, None] * visit[None, :]
    cube = density.reshape(count, count, size, size, size)
    freq = jnp.fft.fftn(cube, axes=(2, 3, 4))
    potential = jnp.real(jnp.fft.ifftn(freq * kernel, axes=(2, 3, 4)))
    potential = potential.reshape(count, count, size, size * size).astype(jnp.float32)
    home_term = -jnp.sum(visit_occ[None, :, None, None] * visit[None, :] * potential, axis=1)
    visit_term = -jnp.sum(home_occ[:, None, None, None] * home[:, None] * potential, axis=0)
    return home_term, visit_term


def reference(orbitals, occupation):
    size = orbitals.shape[1]
    count = ORB_DEV
    blocks = orbitals.reshape(N_GROUP * N_BLK, count, size, size * size)
    occ_blocks = occupation.reshape(N_GROUP * N_BLK, count)
    kernel = make_kernel(size)

    def one_block(acc, home_index):
        group_index = home_index // N_BLK
        place = home_index % N_BLK
        home = blocks[home_index]
        home_occ = occ_blocks[home_index]
        partners = []
        for shift in range(1, STEPS + 1):
            partners.append(group_index * N_BLK + (place - shift) % N_BLK)
        partners.append(((group_index - 1) % N_GROUP) * N_BLK + (place - STEPS) % N_BLK)
        for partner in partners:
            partner = partner.astype(jnp.int32)
            visit = blocks[partner]
            visit_occ = occ_blocks[partner]
            home_term, visit_term = pair_terms(home, home_occ, visit, visit_occ, kernel)
            acc = acc.at[home_index].add(home_term)
            acc = acc.at[partner].add(visit_term)
        return acc, None

    start = jnp.zeros(blocks.shape, jnp.float32)
    result, _ = lax.scan(one_block, start, jnp.arange(N_GROUP * N_BLK, dtype=jnp.int32))
    return result.reshape(orbitals.shape)
```

```python
import functools

import jax
import jax.numpy as jnp
import numpy as np
from jax import lax
from jax.experimental import pallas as pl
from jax.experimental.pallas import tpu as pltpu
from jax.sharding import PartitionSpec as P


def real_basis(size):
    x = np.arange(size)
    rows, square = [np.full(size, np.sqrt(1.0 / size))], [0]
    for m in range(1, size // 2):
        angle = 2.0 * np.pi * (m * x % size) / size
        rows.append(np.sqrt(2.0 / size) * np.cos(angle))
        rows.append(np.sqrt(2.0 / size) * np.sin(angle))
        square += [m * m, m * m]
    rows.append(np.sqrt(1.0 / size) * np.where(x % 2 == 0, 1.0, -1.0))
    square.append((size // 2) ** 2)
    return np.stack(rows), np.array(square)


def split(x):
    hi = x.astype(jnp.bfloat16)
    return hi, (x - hi.astype(jnp.float32)).astype(jnp.bfloat16)


def left_table(q):
    hi = q.astype(jnp.bfloat16)
    lo = (q - hi.astype(np.float32)).astype(jnp.bfloat16)
    return np.concatenate([hi, hi, lo], axis=1)


def right_table(q):
    hi = q.astype(jnp.bfloat16)
    lo = (q - hi.astype(np.float32)).astype(jnp.bfloat16)
    return np.concatenate([hi, hi, lo], axis=0)


@functools.cache
def make_tables(size):
    half = size // 2
    basis, square = real_basis(size)
    odd = np.sqrt(square).astype(np.int64) % 2 == 1
    even_rows, odd_rows = np.where(~odd)[0], np.where(odd)[0]
    b_even, b_odd = basis[even_rows][:, :half], basis[odd_rows][:, :half]
    lanes = np.kron(np.array([[1.0, 1.0], [1.0, -1.0]]), basis.T)
    f32 = np.float32
    wl = right_table(lanes.astype(f32))
    wli = right_table(lanes.T.astype(f32))
    b_fwd = left_table(np.concatenate([b_even, b_odd], axis=0).astype(f32))
    b_inv = left_table(np.concatenate([b_even.T, b_odd.T], axis=0).astype(f32))
    a_fwd = left_table(basis.astype(f32))
    a_inv = left_table(basis.T.astype(f32))
    step = 2.0 * np.pi / size
    sq_b = np.stack([square[even_rows], square[odd_rows]], axis=1)
    total = (
        square[None, :, None, None] + sq_b[:, None, :, None] + square[None, None, None, :]
    )
    kern = (np.pi / (step * step * total + 0.25)).astype(f32)
    kern = kern.reshape(half, size, 2 * size)
    return wl, wli, b_fwd, b_inv, a_fwd, a_inv, kern


def stack3(x):
    hi, lo = split(x)
    return jnp.concatenate([hi, lo, hi], axis=0)


def dot(a, b):
    return jnp.dot(a, b, preferred_element_type=jnp.float32)


def pair_body(home, visit, acc_in, acc_out, work, tabs):
    wl, wli, b_fwd, b_inv, a_fwd, a_inv, kern = tabs
    size, half, lanes = home.shape
    block = 8

    def lane_product(x, w):
        hi, lo = split(x)
        return dot(jnp.concatenate([hi, lo, hi], axis=1), w)

    low = lax.broadcasted_iota(jnp.int32, (half, 2 * lanes), 1) % lanes < lanes // 2

    def b_product(rows, table):
        out = []
        for k in range(0, block, 2):
            x = jnp.concatenate(
                [rows[k * half:(k + 1) * half], rows[(k + 1) * half:(k + 2) * half]], axis=1
            )
            y = dot(table, stack3(x))
            y = jnp.where(low, y[:half], y[half:])
            out += [y[:, :lanes], y[:, lanes:]]
        return jnp.concatenate(out, axis=0)

    @pl.loop(0, size // block)
    def _(i):
        at = pl.ds(pl.multiple_of(i * block, block), block)
        x = (home[at] * visit[at]).reshape(block * half, lanes)
        x = lane_product(x, wl[...])
        x = b_product(x, b_fwd[...])
        work[pl.ds(pl.multiple_of(i * block * half, block * half), block * half)] = x

    group = 4

    @pl.loop(0, half // group)
    def _(i):
        x = jnp.concatenate(
            [work[pl.ds(i * group + k, size, stride=half)] for k in range(group)], axis=1
        )
        scale = jnp.concatenate([kern[i * group + k] for k in range(group)], axis=1)
        x = dot(a_fwd[...], stack3(x)) * scale
        x = dot(a_inv[...], stack3(x))
        for k in range(group):
            work[pl.ds(i * group + k, size, stride=half)] = x[:, k * lanes:(k + 1) * lanes]

    @pl.loop(0, size // block)
    def _(i):
        at = pl.ds(pl.multiple_of(i * block, block), block)
        x = work[pl.ds(pl.multiple_of(i * block * half, block * half), block * half)]
        x = b_product(x, b_inv[...])
        x = lane_product(x, wli[...]).reshape(block, half, lanes)
        term = visit[at] * x
        if acc_in is None:
            acc_out[at] = -term
        else:
            acc_out[at] = acc_in[at] - term


def pairs_kernel(count, has_acc, *refs):
    home, visits = refs[0], refs[1:1 + count]
    acc_in = refs[1 + count] if has_acc else None
    tabs = refs[1 + count + has_acc:8 + count + has_acc]
    out, work = refs[8 + count + has_acc:]
    for k in range(count):
        pair_body(home, visits[k], out if k else acc_in, out, work, tabs)


def meet(home, visits, acc, tabs):
    size, half, lanes = home.shape
    count, has_acc = len(visits), int(acc is not None)
    args = [home, *visits] + ([acc] if has_acc else []) + list(tabs)
    return pl.pallas_call(
        functools.partial(pairs_kernel, count, has_acc),
        out_shape=jax.ShapeDtypeStruct(home.shape, jnp.float32),
        in_specs=[pl.BlockSpec(memory_space=pltpu.VMEM)] * len(args),
        out_specs=pl.BlockSpec(memory_space=pltpu.VMEM),
        scratch_shapes=[pltpu.VMEM((size * half, lanes), jnp.float32)],
        compiler_params=pltpu.CompilerParams(vmem_limit_bytes=32 * 2**20),
        cost_estimate=pl.CostEstimate(
            flops=count * 3 * 10**9, bytes_accessed=4 * home.size * (2 + count), transcendentals=0
        ),
    )(*args)


def local(groups, blks, orbitals, occupation):
    size = orbitals.shape[1]
    half = size // 2
    tabs = [jnp.asarray(t) for t in make_tables(size)]
    names = ("group", "blk")
    zs = blks // 2

    def holder(g, b):
        return (g // 2 * 2 + b % 2) * blks + b // 2 * 2 + g % 2

    def send(value, target):
        moves = []
        for g in range(groups):
            for z in range(zs):
                for c in range(2):
                    tg, tz, tc = target(g, z, c)
                    moves.append(
                        (holder(g, 2 * z + c), holder(tg % groups, tz % zs * 2 + tc))
                    )
        return lax.ppermute(value, names, moves)

    swap = [(g * blks + b, holder(g, b)) for g in range(groups) for b in range(blks)]
    core = lax.axis_index("group") % 2

    home = orbitals[0].reshape(size, 2, half, size).transpose(0, 2, 1, 3)
    home = home.reshape(size, half, 2 * size)
    weight = jnp.sqrt(occupation[0])
    home = lax.ppermute(home * weight, names, swap)

    up = send(home, lambda g, z, c: (g, z + 1, c))
    down = send(home, lambda g, z, c: (g, z - 1, c))
    side = send(home, lambda g, z, c: (g, z, 1 - c))
    far = send(
        jnp.where(core == 1, up, down),
        lambda g, z, c: (g, z + (1 if c == 1 else -1), 1 - c),
    )
    up_side = send(up, lambda g, z, c: (g, z, 1 - c))
    down_side = send(down, lambda g, z, c: (g, z, 1 - c))
    cross_near = send(
        jnp.where(core == 0, down_side, up_side),
        lambda g, z, c: (g + (1 if c == 1 else -1), z, c),
    )
    cross_far = send(far, lambda g, z, c: (g + (1 if c == 0 else -1), z, c))

    acc = meet(home, [side], None, tabs)
    acc = meet(home, [up, down], acc, tabs)
    acc = meet(home, [up_side, down_side], acc, tabs)
    acc = meet(home, [far, cross_near], acc, tabs)
    acc = meet(home, [cross_far], acc, tabs)
    acc = lax.ppermute(acc, names, [(t, s) for s, t in swap]) / weight
    acc = acc.reshape(size, half, 2, size).transpose(0, 2, 1, 3)
    return acc.reshape(1, size, size * size)


def solution(mesh):
    return jax.shard_map(
        functools.partial(local, mesh.shape["group"], mesh.shape["blk"]),
        mesh=mesh,
        in_specs=(P(("group", "blk"), None, None), P(("group", "blk"))),
        out_specs=P(("group", "blk"), None, None),
        check_vma=False,
    )
```

```python
import functools

import jax
import jax.numpy as jnp
import numpy as np
from jax import lax
from jax.experimental import pallas as pl
from jax.experimental.pallas import tpu as pltpu
from jax.sharding import PartitionSpec as P


BLOCK, GROUP, WIDE = 64, 32, 2


def real_basis(size):
    x = np.arange(size)
    rows, square = [np.full(size, np.sqrt(1.0 / size))], [0]
    for m in range(1, size // 2):
        angle = 2.0 * np.pi * (m * x % size) / size
        rows.append(np.sqrt(2.0 / size) * np.cos(angle))
        rows.append(np.sqrt(2.0 / size) * np.sin(angle))
        square += [m * m, m * m]
    rows.append(np.sqrt(1.0 / size) * np.where(x % 2 == 0, 1.0, -1.0))
    square.append((size // 2) ** 2)
    return np.stack(rows), np.array(square)


def split(x):
    hi = x.astype(jnp.bfloat16)
    return hi, (x - hi.astype(jnp.float32)).astype(jnp.bfloat16)


def left_table(q):
    hi = q.astype(jnp.bfloat16)
    lo = (q - hi.astype(np.float32)).astype(jnp.bfloat16)
    return np.concatenate([hi, hi, lo], axis=1)


def right_table(q):
    hi = q.astype(jnp.bfloat16)
    lo = (q - hi.astype(np.float32)).astype(jnp.bfloat16)
    return np.concatenate([hi, hi, lo], axis=0)


@functools.cache
def make_tables(size):
    half = size // 2
    basis, square = real_basis(size)
    odd = np.sqrt(square).astype(np.int64) % 2 == 1
    even_rows, odd_rows = np.where(~odd)[0], np.where(odd)[0]
    b_even, b_odd = basis[even_rows][:, :half], basis[odd_rows][:, :half]
    lanes = np.kron(np.array([[1.0, 1.0], [1.0, -1.0]]), basis.T)
    f32 = np.float32
    wl = right_table(lanes.astype(f32))
    wli = right_table(lanes.T.astype(f32))
    b_fwd = left_table(np.concatenate([b_even, b_odd], axis=0).astype(f32))
    b_inv = left_table(np.concatenate([b_even.T, b_odd.T], axis=0).astype(f32))
    a_fwd = left_table(basis.astype(f32))
    a_inv = left_table(basis.T.astype(f32))
    step = 2.0 * np.pi / size
    sq_b = np.stack([square[even_rows], square[odd_rows]], axis=1)
    total = (
        square[None, :, None, None] + sq_b[:, None, :, None] + square[None, None, None, :]
    )
    kern = (np.pi / (step * step * total + 0.25)).astype(f32)
    kern = kern.reshape(half, size, 2 * size)
    return wl, wli, b_fwd, b_inv, a_fwd, a_inv, kern


def stack3(x):
    hi, lo = split(x)
    return jnp.concatenate([hi, lo, hi], axis=0)


def dot(a, b):
    return jnp.dot(a, b, preferred_element_type=jnp.float32)


def pair_body(home, visit, acc_in, acc_out, work, tabs):
    wl, wli, b_fwd, b_inv, a_fwd, a_inv, kern = tabs
    size, half, lanes = home.shape
    block = BLOCK

    def lane_product(x, w):
        hi, lo = split(x)
        return dot(jnp.concatenate([hi, lo, hi], axis=1), w)

    low = lax.broadcasted_iota(jnp.int32, (half, WIDE * lanes), 1) % lanes < lanes // 2

    def b_product(rows, table):
        out = []
        for k in range(0, block, WIDE):
            x = jnp.concatenate(
                [rows[(k + j) * half:(k + j + 1) * half] for j in range(WIDE)], axis=1
            )
            y = dot(table, stack3(x))
            y = jnp.where(low, y[:half], y[half:])
            out += [y[:, j * lanes:(j + 1) * lanes] for j in range(WIDE)]
        return jnp.concatenate(out, axis=0)

    @pl.loop(0, size // block)
    def _(i):
        at = pl.ds(pl.multiple_of(i * block, block), block)
        x = (home[at] * visit[at]).reshape(block * half, lanes)
        x = lane_product(x, wl[...])
        x = b_product(x, b_fwd[...])
        work[pl.ds(pl.multiple_of(i * block * half, block * half), block * half)] = x

    group = GROUP

    @pl.loop(0, half // group)
    def _(i):
        x = jnp.concatenate(
            [work[pl.ds(i * group + k, size, stride=half)] for k in range(group)], axis=1
        )
        scale = jnp.concatenate([kern[i * group + k] for k in range(group)], axis=1)
        x = dot(a_fwd[...], stack3(x)) * scale
        x = dot(a_inv[...], stack3(x))
        for k in range(group):
            work[pl.ds(i * group + k, size, stride=half)] = x[:, k * lanes:(k + 1) * lanes]

    @pl.loop(0, size // block)
    def _(i):
        at = pl.ds(pl.multiple_of(i * block, block), block)
        x = work[pl.ds(pl.multiple_of(i * block * half, block * half), block * half)]
        x = b_product(x, b_inv[...])
        x = lane_product(x, wli[...]).reshape(block, half, lanes)
        term = visit[at] * x
        if acc_in is None:
            acc_out[at] = -term
        else:
            acc_out[at] = acc_in[at] - term


FIRST, SECOND, SIDE, FIRST_SIDE, SECOND_SIDE, FAR, CROSS_NEAR, CROSS_FAR = range(8)
SLOTS = 8


def exchange_kernel(groups, zs, home, *refs):
    tabs, (out, buf, work, send_sem, recv_sem) = refs[:7], refs[7:]
    group, blk = lax.axis_index("group"), lax.axis_index("blk")
    core, z = group % 2, blk // 2
    g = group // 2 * 2 + blk % 2
    turn = 2 * core - 1

    def device(tg, tz, tc):
        tg = (tg + groups) % groups
        tz = (tz + zs) % zs
        return (tg // 2 * 2 + tc, tz * 2 + tg % 2)

    goes = {
        FIRST: device(g, z + turn, core),
        SECOND: device(g, z - turn, core),
        SIDE: device(g, z, 1 - core),
        FIRST_SIDE: device(g, z, 1 - core),
        SECOND_SIDE: device(g, z, 1 - core),
        FAR: device(g, z + turn, 1 - core),
        CROSS_NEAR: device(g + turn, z, core),
        CROSS_FAR: device(g - turn, z, core),
    }
    barrier = pltpu.get_barrier_semaphore()
    peers = [goes[FIRST], goes[SECOND], goes[SIDE], goes[CROSS_NEAR], goes[CROSS_FAR]]
    peers += [goes[FAR]]
    for peer in peers:
        pl.semaphore_signal(barrier, inc=1, device_id=peer, device_id_type=pl.DeviceIdType.MESH)
    pl.semaphore_wait(barrier, len(peers))

    def copy(source, slot):
        return pltpu.make_async_remote_copy(
            src_ref=source,
            dst_ref=buf.at[slot],
            send_sem=send_sem.at[slot],
            recv_sem=recv_sem.at[slot],
            device_id=goes[slot],
            device_id_type=pl.DeviceIdType.MESH,
        )

    copies = {
        FIRST: copy(home, FIRST),
        SECOND: copy(home, SECOND),
        SIDE: copy(home, SIDE),
        FIRST_SIDE: copy(buf.at[FIRST], FIRST_SIDE),
        SECOND_SIDE: copy(buf.at[SECOND], SECOND_SIDE),
        FAR: copy(buf.at[FIRST], FAR),
        CROSS_NEAR: copy(buf.at[SECOND_SIDE], CROSS_NEAR),
        CROSS_FAR: copy(buf.at[FAR], CROSS_FAR),
    }

    def meet(slot, first=False):
        pair_body(home, buf.at[slot], None if first else out, out, work, tabs)

    copies[FIRST].start()
    copies[SIDE].start()
    copies[SECOND].start()
    copies[SIDE].wait_recv()
    meet(SIDE, True)
    copies[FIRST].wait_recv()
    copies[FAR].start()
    copies[FIRST_SIDE].start()
    meet(FIRST)
    copies[SECOND].wait_recv()
    copies[SECOND_SIDE].start()
    meet(SECOND)
    copies[SECOND_SIDE].wait_recv()
    copies[CROSS_NEAR].start()
    copies[FIRST_SIDE].wait_recv()
    copies[FAR].wait_recv()
    copies[CROSS_FAR].start()

    @pl.loop(FIRST_SIDE, CROSS_NEAR)
    def _(slot):
        meet(slot)

    copies[CROSS_NEAR].wait_recv()
    copies[CROSS_FAR].wait_recv()

    @pl.loop(CROSS_NEAR, SLOTS)
    def _(slot):
        meet(slot)

    for slot in range(SLOTS):
        copies[slot].wait_send()


def exchange(groups, zs, home, tabs):
    size, half, lanes = home.shape
    vmem = pl.BlockSpec(memory_space=pltpu.VMEM)
    return pl.pallas_call(
        functools.partial(exchange_kernel, groups, zs),
        out_shape=jax.ShapeDtypeStruct(home.shape, jnp.float32),
        in_specs=[vmem] * 8,
        out_specs=vmem,
        scratch_shapes=[
            pltpu.VMEM((SLOTS, size, half, lanes), jnp.float32),
            pltpu.VMEM((size * half, lanes), jnp.float32),
            pltpu.SemaphoreType.DMA((SLOTS,)),
            pltpu.SemaphoreType.DMA((SLOTS,)),
        ],
        compiler_params=pltpu.CompilerParams(
            vmem_limit_bytes=40 * 2**20, collective_id=0, has_side_effects=True
        ),
        cost_estimate=pl.CostEstimate(
            flops=24 * 10**9, bytes_accessed=8 * home.size, transcendentals=0
        ),
    )(home, *tabs)


def local(groups, blks, orbitals, occupation):
    size = orbitals.shape[1]
    half = size // 2
    tabs = [jnp.asarray(t) for t in make_tables(size)]
    names = ("group", "blk")

    def holder(g, b):
        return (g // 2 * 2 + b % 2) * blks + b // 2 * 2 + g % 2

    swap = [(g * blks + b, holder(g, b)) for g in range(groups) for b in range(blks)]
    home = orbitals[0].reshape(size, 2, half, size).transpose(0, 2, 1, 3)
    home = home.reshape(size, half, 2 * size)
    weight = jnp.sqrt(occupation[0])
    home = lax.ppermute(home * weight, names, swap)
    acc = exchange(groups, blks // 2, home, tabs)
    acc = lax.ppermute(acc, names, [(t, s) for s, t in swap]) / weight
    acc = acc.reshape(size, half, 2, size).transpose(0, 2, 1, 3)
    return acc.reshape(1, size, size * size)


def solution(mesh):
    return jax.shard_map(
        functools.partial(local, mesh.shape["group"], mesh.shape["blk"]),
        mesh=mesh,
        in_specs=(P(("group", "blk"), None, None), P(("group", "blk"))),
        out_specs=P(("group", "blk"), None, None),
        check_vma=False,
    )
```

```python
import functools

import jax
import jax.numpy as jnp
import numpy as np
from jax import lax
from jax.experimental import pallas as pl
from jax.experimental.pallas import tpu as pltpu
from jax.sharding import PartitionSpec as P


BLOCK, GROUP, WIDE = 64, 32, 2


def real_basis(size):
    x = np.arange(size)
    rows, square = [np.full(size, np.sqrt(1.0 / size))], [0]
    for m in range(1, size // 2):
        angle = 2.0 * np.pi * (m * x % size) / size
        rows.append(np.sqrt(2.0 / size) * np.cos(angle))
        rows.append(np.sqrt(2.0 / size) * np.sin(angle))
        square += [m * m, m * m]
    rows.append(np.sqrt(1.0 / size) * np.where(x % 2 == 0, 1.0, -1.0))
    square.append((size // 2) ** 2)
    return np.stack(rows), np.array(square)


def split(x):
    hi = x.astype(jnp.bfloat16)
    return hi, (x - hi.astype(jnp.float32)).astype(jnp.bfloat16)


def left_table(q):
    hi = q.astype(jnp.bfloat16)
    lo = (q - hi.astype(np.float32)).astype(jnp.bfloat16)
    return np.concatenate([hi, hi, lo], axis=1)


def right_table(q):
    hi = q.astype(jnp.bfloat16)
    lo = (q - hi.astype(np.float32)).astype(jnp.bfloat16)
    return np.concatenate([hi, hi, lo], axis=0)


@functools.cache
def make_tables(size):
    half = size // 2
    basis, square = real_basis(size)
    odd = np.sqrt(square).astype(np.int64) % 2 == 1
    even_rows, odd_rows = np.where(~odd)[0], np.where(odd)[0]
    b_even, b_odd = basis[even_rows][:, :half], basis[odd_rows][:, :half]
    lanes = np.kron(np.array([[1.0, 1.0], [1.0, -1.0]]), basis.T)
    f32 = np.float32
    wl = right_table(lanes.astype(f32))
    wli = right_table(lanes.T.astype(f32))
    b_fwd = left_table(np.concatenate([b_even, b_odd], axis=0).astype(f32))
    b_inv = left_table(np.concatenate([b_even.T, b_odd.T], axis=0).astype(f32))
    a_fwd = left_table(basis.astype(f32))
    a_inv = left_table(basis.T.astype(f32))
    step = 2.0 * np.pi / size
    sq_b = np.stack([square[even_rows], square[odd_rows]], axis=1)
    total = (
        square[None, :, None, None] + sq_b[:, None, :, None] + square[None, None, None, :]
    )
    kern = (np.pi / (step * step * total + 0.25)).astype(f32)
    kern = kern.reshape(half, size, 2 * size)
    return wl, wli, b_fwd, b_inv, a_fwd, a_inv, kern


def stack3(x):
    hi, lo = split(x)
    return jnp.concatenate([hi, lo, hi], axis=0)


def dot(a, b):
    return jnp.dot(a, b, preferred_element_type=jnp.float32)


def pair_body(home, visit, acc_in, acc_out, work, tabs):
    wl, wli, b_fwd, b_inv, a_fwd, a_inv, kern = tabs
    size, half, lanes = home.shape
    block = BLOCK

    def lane_product(x, w):
        hi, lo = split(x)
        return dot(jnp.concatenate([hi, lo, hi], axis=1), w)

    low = lax.broadcasted_iota(jnp.int32, (half, WIDE * lanes), 1) % lanes < lanes // 2

    def b_product(rows, table):
        out = []
        for k in range(0, block, WIDE):
            x = jnp.concatenate(
                [rows[(k + j) * half:(k + j + 1) * half] for j in range(WIDE)], axis=1
            )
            y = dot(table, stack3(x))
            y = jnp.where(low, y[:half], y[half:])
            out += [y[:, j * lanes:(j + 1) * lanes] for j in range(WIDE)]
        return jnp.concatenate(out, axis=0)

    @pl.loop(0, size // block)
    def _(i):
        at = pl.ds(pl.multiple_of(i * block, block), block)
        x = (home[at] * visit[at]).reshape(block * half, lanes)
        x = lane_product(x, wl[...])
        x = b_product(x, b_fwd[...])
        work[pl.ds(pl.multiple_of(i * block * half, block * half), block * half)] = x

    group = GROUP

    @pl.loop(0, half // group)
    def _(i):
        x = jnp.concatenate(
            [work[pl.ds(i * group + k, size, stride=half)] for k in range(group)], axis=1
        )
        scale = jnp.concatenate([kern[i * group + k] for k in range(group)], axis=1)
        x = dot(a_fwd[...], stack3(x)) * scale
        x = dot(a_inv[...], stack3(x))
        for k in range(group):
            work[pl.ds(i * group + k, size, stride=half)] = x[:, k * lanes:(k + 1) * lanes]

    @pl.loop(0, size // block)
    def _(i):
        at = pl.ds(pl.multiple_of(i * block, block), block)
        x = work[pl.ds(pl.multiple_of(i * block * half, block * half), block * half)]
        x = b_product(x, b_inv[...])
        x = lane_product(x, wli[...]).reshape(block, half, lanes)
        term = visit[at] * x
        if acc_in is None:
            acc_out[at] = -term
        else:
            acc_out[at] = acc_in[at] - term


SIDE, FIRST, FIRST_SIDE, FAR, SECOND, SECOND_SIDE, CROSS_FAR, CROSS_NEAR = range(8)
SLOTS = 8
PARTS = 2


def exchange_kernel(groups, zs, home, *refs):
    tabs, (out, buf, work, send_sem, recv_sem) = refs[:7], refs[7:]
    group, blk = lax.axis_index("group"), lax.axis_index("blk")
    core, z = group % 2, blk // 2
    g = group // 2 * 2 + blk % 2
    turn = 2 * core - 1

    def device(tg, tz, tc):
        tg = (tg + groups) % groups
        tz = (tz + zs) % zs
        return (tg // 2 * 2 + tc, tz * 2 + tg % 2)

    goes = {
        FIRST: device(g, z + turn, core),
        SECOND: device(g, z - turn, core),
        SIDE: device(g, z, 1 - core),
        FIRST_SIDE: device(g, z, 1 - core),
        SECOND_SIDE: device(g, z, 1 - core),
        FAR: device(g, z + turn, 1 - core),
        CROSS_NEAR: device(g - turn, z, 1 - core),
        CROSS_FAR: device(g - turn, z, core),
    }
    barrier = pltpu.get_barrier_semaphore()
    peers = [goes[slot] for slot in (FIRST, SECOND, SIDE, FAR, CROSS_NEAR, CROSS_FAR)]
    peers.append(device(g + turn, z, core))
    for peer in peers:
        pl.semaphore_signal(barrier, inc=1, device_id=peer, device_id_type=pl.DeviceIdType.MESH)
    pl.semaphore_wait(barrier, len(peers))

    rows = home.shape[0] // PARTS

    def copy(source, slot, part):
        at = pl.ds(part * rows, rows)
        return pltpu.make_async_remote_copy(
            src_ref=source.at[at],
            dst_ref=buf.at[slot, at],
            send_sem=send_sem.at[slot, part],
            recv_sem=recv_sem.at[slot, part],
            device_id=goes[slot],
            device_id_type=pl.DeviceIdType.MESH,
        )

    sources = {
        FIRST: home,
        SECOND: home,
        SIDE: home,
        FIRST_SIDE: buf.at[FIRST],
        SECOND_SIDE: buf.at[SECOND],
        FAR: buf.at[FIRST],
        CROSS_NEAR: buf.at[SECOND],
        CROSS_FAR: buf.at[FAR],
    }
    copies = {
        slot: [copy(source, slot, part) for part in range(PARTS)]
        for slot, source in sources.items()
    }

    def start(slot):
        for part in copies[slot]:
            part.start()

    def arrive(slot):
        for part in copies[slot]:
            part.wait_recv()

    def relay(slot, *onward):
        for part in range(PARTS):
            copies[slot][part].wait_recv()
            for to in onward:
                copies[to][part].start()

    def meet(slot, first=False):
        pair_body(home, buf.at[slot], None if first else out, out, work, tabs)

    start(FIRST)
    start(SIDE)
    arrive(SIDE)
    meet(SIDE, True)
    relay(FIRST, FAR)
    start(SECOND)
    start(FIRST_SIDE)
    meet(FIRST)
    arrive(FIRST_SIDE)
    meet(FIRST_SIDE)
    relay(FAR, CROSS_FAR)
    meet(FAR)
    relay(SECOND, CROSS_NEAR, SECOND_SIDE)
    arrive(SECOND_SIDE)

    @pl.loop(SECOND, CROSS_FAR)
    def _(slot):
        meet(slot)

    arrive(CROSS_FAR)
    arrive(CROSS_NEAR)

    @pl.loop(CROSS_FAR, SLOTS)
    def _(slot):
        meet(slot)

    for slot in range(SLOTS):
        for part in copies[slot]:
            part.wait_send()


def exchange(groups, zs, home, tabs):
    size, half, lanes = home.shape
    vmem = pl.BlockSpec(memory_space=pltpu.VMEM)
    return pl.pallas_call(
        functools.partial(exchange_kernel, groups, zs),
        out_shape=jax.ShapeDtypeStruct(home.shape, jnp.float32),
        in_specs=[vmem] * 8,
        out_specs=vmem,
        scratch_shapes=[
            pltpu.VMEM((SLOTS, size, half, lanes), jnp.float32),
            pltpu.VMEM((size * half, lanes), jnp.float32),
            pltpu.SemaphoreType.DMA((SLOTS, PARTS)),
            pltpu.SemaphoreType.DMA((SLOTS, PARTS)),
        ],
        compiler_params=pltpu.CompilerParams(
            vmem_limit_bytes=40 * 2**20, collective_id=0, has_side_effects=True
        ),
        cost_estimate=pl.CostEstimate(
            flops=24 * 10**9, bytes_accessed=8 * home.size, transcendentals=0
        ),
    )(home, *tabs)


def local(groups, blks, orbitals, occupation):
    size = orbitals.shape[1]
    half = size // 2
    tabs = [jnp.asarray(t) for t in make_tables(size)]
    names = ("group", "blk")

    def holder(g, b):
        return (g // 2 * 2 + b % 2) * blks + b // 2 * 2 + g % 2

    swap = [(g * blks + b, holder(g, b)) for g in range(groups) for b in range(blks)]
    home = orbitals[0].reshape(size, 2, half, size).transpose(0, 2, 1, 3)
    home = home.reshape(size, half, 2 * size)
    weight = jnp.sqrt(occupation[0])
    home = lax.ppermute(home * weight, names, swap)
    acc = exchange(groups, blks // 2, home, tabs)
    acc = lax.ppermute(acc, names, [(t, s) for s, t in swap]) / weight
    acc = acc.reshape(size, half, 2, size).transpose(0, 2, 1, 3)
    return acc.reshape(1, size, size * size)


def solution(mesh):
    return jax.shard_map(
        functools.partial(local, mesh.shape["group"], mesh.shape["blk"]),
        mesh=mesh,
        in_specs=(P(("group", "blk"), None, None), P(("group", "blk"))),
        out_specs=P(("group", "blk"), None, None),
        check_vma=False,
    )
```
